32 devices in a mesh: req: 8 (over z, x), tp: 4 (over y, core).
Axes of the slice: x: 2, y: 2, z: 4, core: 2. Of those that a mesh axis runs over, the one named last changes fastest.
Arguments:
- queries: bfloat16 [2, 8, 32, 1536], P(None, 'req', None, 'tp')
- response_kv: bfloat16 [2, 8, 2, 32, 256], P(None, 'req'), may hold values from -6 to 6
- cache_kv: bfloat16 [2, 8, 2, 384, 256], P(None, 'req'), may hold values from -6 to 6
- residual: bfloat16 [2, 8, 32, 1536], P(None, 'req')
- out_proj: bfloat16 [2, 1536, 1536], P(None, 'tp'), may hold values from -0.5 to 0.5
- norm_gain: float32 [2, 1536], replicated, may hold values from 0.25 to 1.75
- lm_head: bfloat16 [2, 8192, 1536], P(None, 'req', 'tp')
- targets: int32 [8, 32], P(None, 'tp'), may hold values from 0 to 8191
- resp_lengths: int32 [8], replicated, may hold values from 1 to 32, 160 in all
- cache_lengths: int32 [8], P('req'), may hold values from 1 to 384, 1920 in all
- owner_slot: int32 [8], replicated, may hold values from 0 to 7, each once
- sink_count: int32 [1], replicated, may hold values from 1 to 95
- window_size: int32 [1], replicated, may hold values from 48 to 191
Outputs:
- token_logprobs: float32 [8, 32], P('req', 'tp')
- request_scores: float32 [8, 2], P('req')
The draws below stay inside these ranges and needn't reach their ends.
Inputs may be any that keep to these rules, and one draw needn't show every extreme that they name: `resp_lengths`: live response slots are the first ones; all lengths sum to 160. `cache_lengths`: live cache slots are the first ones; all lengths sum to 1920. `owner_slot`: A permutation of the requests.
All inputs are finite; a program needn't handle non-finite values. No bound on the sum of `cache_lengths` on one device may be relied on, other than what follows from the above.
Results may differ from the reference program's by a relative error of at most 0.0014.
Values may be sent and summed in bfloat16 or wider, within the bound.
No kernel may reach another device: no remote copies, remote signals or barrier semaphores. Data moves between devices by JAX's collectives and lax.ppermute only.
A program may use at most 128 MiB of HBM per device.

```python
import math
import jax
import jax.numpy as jnp
import numpy as np
from jax import lax

D = 1536
HEADS = 12
HEAD = 128
KV_HEADS = 2
VOCAB_REQ = 1024
RESP = 32
CACHE = 384
REQS = 8
VOCAB = 8192
N_REQ = 8


def draw_residual(key, part):
    key_base, key_rows, key_cols = jax.random.split(key, 3)
    base_value = jnp.clip(jax.random.normal(key_base, (2, REQS, RESP, D), jnp.float32), -6.0, 6.0)
    row_low = 0.3
    row_high = 3.0
    row_scale = jnp.exp(jax.random.uniform(key_rows, (2, REQS, RESP, 1), jnp.float32, math.log(row_low), math.log(row_high)))
    col_scale = jnp.exp(jax.random.uniform(key_cols, (2, 1, 1, D), jnp.float32, math.log(0.3), math.log(3.0)))
    return (base_value * row_scale * col_scale).astype(jnp.bfloat16)


def draw_queries(key, part):
    key_base = jax.random.fold_in(key, 0)
    base_value = jnp.clip(jax.random.normal(key_base, (2, REQS, RESP, HEADS, HEAD), jnp.float32), -6.0, 6.0)
    return base_value.reshape(2, REQS, RESP, HEADS * HEAD).astype(jnp.bfloat16)


def draw_lm_head(key, part):
    key_base = jax.random.fold_in(key, 0)
    base_value = jnp.clip(jax.random.normal(key_base, (2, VOCAB, D), jnp.float32), -6.0, 6.0) * (3.0 / math.sqrt(D))
    return base_value.astype(jnp.bfloat16)


def with_ends(values, own_key, smallest, top_value):
    index_at = [jax.random.randint(jax.random.fold_in(own_key, axis), (), 0, length) for axis, length in enumerate(values.shape)]
    main_axis = values.shape.index(max(values.shape))
    neighbour = index_at[:main_axis] + [(index_at[main_axis] + 1) % values.shape[main_axis]] + index_at[main_axis + 1:]
    return values.at[tuple(index_at)].set(smallest).at[tuple(neighbour)].set(top_value)


def block_scale(own_key, dims, cuts, low, largest):
    gain = 1.0
    for position, parts in cuts:
        heights = jax.random.uniform(jax.random.fold_in(jax.random.fold_in(own_key, 6), position), (parts,), jnp.float32, low / len(cuts), largest / len(cuts))
        gain = gain * jnp.repeat(jnp.exp(heights), dims[position] // parts).reshape((-1,) + (1,) * (len(dims) - 1 - position))
    return gain


def profile(count, total, most, skew):
    loads = [(1 << 20) // math.isqrt(rank ** skew) + 1 for rank in range(2, count + 1)]
    surplus, holding = total - most - (count - 1), [1] * (count - 1)
    while surplus > 0:
        movable = [i for i in range(count - 1) if holding[i] < most]
        whole, budget = sum([loads[i] for i in movable]), surplus
        for i in movable:
            more = min(most - holding[i], max(1, budget * loads[i] // whole), surplus)
            holding[i] = holding[i] + more
            surplus = surplus - more
    return np.array([most] + holding)


def uneven_parts(own_key, count, total, limit, lean):
    if count == 2:
        one = jax.random.randint(own_key, (), max(1, total - limit), min(limit, total - 1) + 1)
        return jnp.stack([one, total - one])
    sizes = jnp.asarray(profile(count, total, limit, lean), jnp.int32)
    couples = (count - 1) // 2
    source_of, sink = sizes[1:1 + 2 * couples:2], sizes[2:2 + 2 * couples:2]
    margin = jnp.minimum(source_of - 1, limit - sink)
    passed = jax.random.randint(jax.random.fold_in(own_key, 1), (couples,), 0, 1 << 20) % (margin + 1)
    sizes = sizes.at[1:1 + 2 * couples:2].set(source_of - passed).at[2:2 + 2 * couples:2].set(sink + passed)
    return sizes[jax.random.permutation(jax.random.fold_in(own_key, 2), count)]


def bell_draw(own_key, extent, spread, most, cuts=(), kind=jnp.bfloat16):
    gain = block_scale(own_key, extent, cuts, -0.22, 0.18) if cuts else 1.0
    result = jax.random.normal(own_key, extent, jnp.float32) * spread * gain
    return jnp.minimum(jnp.maximum(result, -most), most).astype(kind)


def setup_inputs(seed: int = 0) -> dict:
    key_of = jax.random.split(jax.random.key(seed), 14)
    return {
        "queries": draw_queries(jax.random.fold_in(key_of[13], 71), 0),
        "response_kv": bell_draw(key_of[1], (2, REQS, 2, RESP, KV_HEADS * HEAD), 1.0, 6.0, ((1, 8),)),
        "cache_kv": bell_draw(key_of[2], (2, REQS, 2, CACHE, KV_HEADS * HEAD), 1.0, 6.0, ((1, 8),)),
        "residual": draw_residual(jax.random.fold_in(key_of[13], 71), 0),
        "out_proj": bell_draw(key_of[4], (2, HEADS * HEAD, D), HEAD ** -0.5, 0.5, ((1, 4),)),
        "norm_gain": jnp.clip(1.0 + 0.15 * jax.random.normal(key_of[5], (2, D), jnp.float32), 0.25, 1.75),
        "lm_head": draw_lm_head(jax.random.fold_in(key_of[13], 71), 0),
        "targets": with_ends(jax.random.randint(key_of[7], (REQS, RESP), 0, VOCAB), jax.random.fold_in(key_of[7], 1), 0, VOCAB - 1).astype(jnp.int32),
        "resp_lengths": uneven_parts(key_of[8], REQS, REQS * RESP * 5 // 8, RESP, 2).astype(jnp.int32),
        "cache_lengths": uneven_parts(key_of[9], REQS, REQS * CACHE * 5 // 8, CACHE, 2).astype(jnp.int32),
        "owner_slot": jax.random.permutation(key_of[10], REQS).astype(jnp.int32),
        "sink_count": jax.random.randint(key_of[11], (1,), 1, CACHE // 4).astype(jnp.int32),
        "window_size": jax.random.randint(key_of[12], (1,), CACHE // 8, CACHE // 2).astype(jnp.int32),
    }


def span_mask(lengths, sink_count, window_size):
    cache_pos = jnp.arange(CACHE, dtype=jnp.int32)
    slot_pos = jnp.arange(RESP, dtype=jnp.int32)
    req_count = lengths.shape[0]
    key_pos = jnp.concatenate([jnp.broadcast_to(cache_pos[None, :], (req_count, CACHE)), lengths[:, None] + slot_pos[None, :]], axis=1)
    key_live = jnp.concatenate([cache_pos[None, :] < lengths[:, None], jnp.ones((req_count, RESP), jnp.bool_)], axis=1)
    query_pos = lengths[:, None] + slot_pos[None, :]
    earlier = key_pos[:, None, :] <= query_pos[:, :, None]
    inside = (key_pos[:, None, :] < sink_count[0]) | (query_pos[:, :, None] - key_pos[:, None, :] < window_size[0])
    return key_live[:, None, :] & earlier & inside

def attend(queries, response_kv, cache_kv, cache_lengths, sink_count, window_size):
    group_size = HEADS // KV_HEADS
    key_span = CACHE + RESP
    query_heads = queries.astype(jnp.float32).reshape(2, REQS, RESP, KV_HEADS, group_size, HEAD)
    key_rows = jnp.concatenate([cache_kv[:, :, 0], response_kv[:, :, 0]], axis=2).astype(jnp.float32).reshape(2, REQS, key_span, KV_HEADS, HEAD)
    value_rows = jnp.concatenate([cache_kv[:, :, 1], response_kv[:, :, 1]], axis=2).astype(jnp.float32).reshape(2, REQS, key_span, KV_HEADS, HEAD)
    scores = jnp.einsum('mrsgjd,mrkgd->mrgjsk', query_heads, key_rows) * HEAD ** (-0.5)
    allowed = span_mask(cache_lengths, sink_count, window_size)[None, :, None, None]
    masked = jnp.where(allowed, scores, -jnp.inf)
    row_peak = lax.optimization_barrier(jnp.max(masked, axis=-1, keepdims=True))
    weights = jnp.exp(masked - row_peak)
    weights = (weights / lax.optimization_barrier(jnp.sum(weights, axis=-1, keepdims=True))).astype(jnp.bfloat16)
    attended = jnp.einsum('mrgjsk,mrkgd->mrsgjd', weights.astype(jnp.float32), value_rows)
    return attended.astype(jnp.bfloat16).reshape(2, REQS, RESP, HEADS * HEAD)

def rms_norm(hidden, norm_gain):
    scale_inv = lax.rsqrt(lax.optimization_barrier(jnp.mean(hidden * hidden, axis=-1, keepdims=True)) + 1e-06)
    return (hidden * scale_inv * norm_gain[:, None, None, :]).astype(jnp.bfloat16)

def vocab_logprob(flat_rows, lm_head, flat_targets):
    rows_wide = flat_rows.astype(jnp.float32)
    row_total = flat_rows.shape[1]
    blocks = lm_head.reshape(2, N_REQ, VOCAB_REQ, D).transpose(1, 0, 2, 3)
    block_starts = jnp.arange(N_REQ, dtype=jnp.int32) * VOCAB_REQ

    def scan_step(running, inputs):
        run_peak, run_total, run_picked = running
        head_block, block_start = inputs
        logits = jnp.einsum('mtd,mvd->mtv', rows_wide, head_block.astype(jnp.float32))
        new_peak = jnp.maximum(run_peak, lax.optimization_barrier(jnp.max(logits, axis=-1)))
        exp_total = run_total * jnp.exp(run_peak - new_peak) + lax.optimization_barrier(jnp.sum(jnp.exp(logits - new_peak[..., None]), axis=-1))
        target_hits = (block_start + jnp.arange(VOCAB_REQ, dtype=jnp.int32))[None, None, :] == flat_targets[None, :, None]
        picked = run_picked + lax.optimization_barrier(jnp.sum(jnp.where(target_hits, logits, 0.0), axis=-1))
        return ((new_peak, exp_total, picked), None)
    initial = (jnp.full((2, row_total), -jnp.inf, jnp.float32), jnp.zeros((2, row_total), jnp.float32), jnp.zeros((2, row_total), jnp.float32))
    final_state, ignored = lax.scan(scan_step, initial, (blocks, block_starts))
    run_peak, run_total, run_picked = final_state
    return run_picked - (run_peak + jnp.log(run_total))

def reference(queries, response_kv, cache_kv, residual, out_proj, norm_gain, lm_head, targets, resp_lengths, cache_lengths, owner_slot, sink_count, window_size):
    attended = attend(queries, response_kv, cache_kv, cache_lengths, sink_count, window_size)
    projected = jnp.einsum('mrsf,mfd->mrsd', attended.astype(jnp.float32), out_proj.astype(jnp.float32))
    hidden = residual.astype(jnp.float32) + projected
    normed = rms_norm(hidden, norm_gain)
    logprob = vocab_logprob(normed.reshape(2, REQS * RESP, D), lm_head, targets.reshape(-1)).reshape(2, REQS, RESP)
    row_order = jnp.zeros((REQS,), jnp.int32).at[owner_slot].set(jnp.arange(REQS, dtype=jnp.int32))
    placed = logprob[:, row_order]
    lengths_placed = resp_lengths[row_order]
    live_slots = jnp.arange(RESP, dtype=jnp.int32)[None, :] < lengths_placed[:, None]
    policy = jnp.where(live_slots, placed[0], 0.0)
    log_ratio = jnp.where(live_slots, placed[0] - placed[1], 0.0)
    counts = lengths_placed.astype(jnp.float32)
    request_scores = jnp.stack([lax.optimization_barrier(jnp.sum(policy, axis=1)) / counts, lax.optimization_barrier(jnp.sum(log_ratio, axis=1)) / counts], axis=1)
    return (policy, request_scores)
```

```python
import functools

import jax
import jax.numpy as jnp
from jax import lax
from jax.experimental import pallas as pl
from jax.experimental.pallas import tpu as pltpu
from jax.sharding import PartitionSpec as P

HEADS = 12
HEAD = 128
KV_HEADS = 2
RESP = 32
CACHE = 384
LANES = 128
MIB = 1 << 20
BRIEF = pl.CostEstimate(flops=1, bytes_accessed=1, transcendentals=0)
VMEM = pl.BlockSpec(memory_space=pltpu.VMEM)
SMEM = pl.BlockSpec(memory_space=pltpu.SMEM)
HBM = pl.BlockSpec(memory_space=pltpu.HBM)


def swap(value, axis, distance):
    size = lax.axis_size(axis)
    return lax.ppermute(value, axis, [(i, i ^ distance) for i in range(size)])


def exchange_steps(size):
    bits = []
    while 2 ** len(bits) < size:
        bits.append(2 ** len(bits))
    groups = [bits[i : i + 2] for i in range(1, len(bits), 2)] + [bits[:1]]
    return [g if len(g) == 1 else [g[0] | g[1], g[1], g[0]] for g in groups]


def gather_order(size):
    order = [0]
    for steps in exchange_steps(size):
        order = order + [step ^ k for step in steps for k in order]
    return order


def offsets_of(lengths, requests):
    starts, running = [], jnp.int32(0)
    for i in range(requests):
        starts.append(running)
        running = running + lengths[i]
    return starts


def attend_kernel(
    tp_size,
    order,
    cache_len,
    sink,
    window,
    lengths_ref,
    owners_ref,
    q_ref,
    targets_ref,
    residual_ref,
    gain_ref,
    resp_ref,
    cache_ref,
    proj_ref,
    send_ref,
    keep_ref,
    own_gain_ref,
    index_ref,
    code_ref,
    span_ref,
    lengths,
    owners,
    q_buf,
    targets_buf,
    residual_buf,
    gain_buf,
    resp_buf,
    cache_buf,
    proj_buf,
    sems,
):
    tp_index = lax.axis_index("tp")
    req_index = lax.axis_index("req")
    requests = len(order)
    heads = HEADS // tp_size
    chunk = proj_ref.shape[2] // tp_size
    quarter = RESP // tp_size
    kv_lane = pl.multiple_of(tp_index * heads // (HEADS // KV_HEADS) * HEAD, HEAD)
    model = tp_index % 2
    own_lane = pl.multiple_of(tp_index // 2 * 2 * chunk, LANES)
    rows_each = proj_ref.shape[1] // 1
    pairs = [
        (cache_ref.at[:, 0, :, :, pl.ds(kv_lane, HEAD)], cache_buf),
        (q_ref.at[:, 0], q_buf),
        (resp_ref.at[:, 0, :, :, pl.ds(kv_lane, HEAD)], resp_buf),
        (residual_ref.at[model, 0, :, pl.ds(own_lane, 2 * chunk)], residual_buf),
        (gain_ref.at[pl.ds(model, 1), pl.ds(own_lane, 2 * chunk)], gain_buf),
        (targets_ref, targets_buf),
        (lengths_ref, lengths),
        (owners_ref, owners),
    ] + [
        (proj_ref.at[m, pl.ds(i * rows_each, rows_each)], proj_buf.at[m, pl.ds(i * rows_each, rows_each)])
        for m in range(2)
        for i in range(1)
    ]
    copies = [
        pltpu.make_async_copy(source, target, sems.at[i])
        for i, (source, target) in enumerate(pairs)
    ]
    for copy in copies:
        copy.start()
    for copy in copies[:3]:
        copy.wait()
    length = cache_len[0]
    rows = heads * RESP
    slot = lax.broadcasted_iota(jnp.int32, (rows, CACHE), 0) % RESP
    key = lax.broadcasted_iota(jnp.int32, (rows, CACHE), 1)
    cache_ok = (key < length) & ((key < sink[0]) | (length + slot - key < window[0]))
    slot = lax.broadcasted_iota(jnp.int32, (rows, RESP), 0) % RESP
    key = lax.broadcasted_iota(jnp.int32, (rows, RESP), 1)
    resp_ok = (key <= slot) & ((length + key < sink[0]) | (slot - key < window[0]))
    contract_last = (((1,), (1,)), ((), ()))
    attended = []
    for m in range(2):
        q = jnp.concatenate([q_buf[m, :, h * HEAD : (h + 1) * HEAD] for h in range(heads)], axis=0)
        cache_score = lax.dot_general(
            q, cache_buf[m, 0], contract_last, preferred_element_type=jnp.float32
        ) * HEAD ** (-0.5)
        resp_score = lax.dot_general(
            q, resp_buf[m, 0], contract_last, preferred_element_type=jnp.float32
        ) * HEAD ** (-0.5)
        cache_score = jnp.where(cache_ok, cache_score, -jnp.inf)
        resp_score = jnp.where(resp_ok, resp_score, -jnp.inf)
        peak = jnp.maximum(
            jnp.max(cache_score, axis=1, keepdims=True), jnp.max(resp_score, axis=1, keepdims=True)
        )
        cache_exp = jnp.exp(cache_score - peak)
        resp_exp = jnp.exp(resp_score - peak)
        total = jnp.sum(cache_exp, axis=1, keepdims=True) + jnp.sum(resp_exp, axis=1, keepdims=True)
        out = jnp.dot(
            (cache_exp / total).astype(jnp.bfloat16), cache_buf[m, 1], preferred_element_type=jnp.float32
        ) + jnp.dot(
            (resp_exp / total).astype(jnp.bfloat16), resp_buf[m, 1], preferred_element_type=jnp.float32
        )
        out = out.astype(jnp.bfloat16)
        attended.append(
            jnp.concatenate([out[h * RESP : (h + 1) * RESP] for h in range(heads)], axis=1)
        )
    for copy in copies[3:]:
        copy.wait()
    own = jnp.where(model == 0, attended[0], attended[1])
    other = jnp.where(model == 0, attended[1], attended[0])
    for k in range(tp_size):
        columns = slice(k * chunk, (k + 1) * chunk)
        for target, rows, m, t in (
            (send_ref, other, 1 - model, tp_index ^ 1 ^ k),
            (keep_ref, own, model, tp_index ^ k),
        ):
            weights = proj_buf[m, :, pl.ds(pl.multiple_of(t * chunk, LANES), chunk)]
            target[0:RESP, columns] = jnp.dot(rows, weights, preferred_element_type=jnp.float32)
    for k in range(2):
        lanes = pl.ds(pl.multiple_of((model ^ k) * chunk, LANES), chunk)
        columns = slice(k * chunk, (k + 1) * chunk)
        keep_ref[0:RESP, columns] += residual_buf[:, lanes].astype(jnp.float32)
        own_gain_ref[:, columns] = gain_buf[:, lanes]
    own_targets = targets_buf[...]
    place = lax.broadcasted_iota(jnp.int32, (quarter, LANES), 1) - tp_index * quarter
    spread = (place == lax.broadcasted_iota(jnp.int32, (quarter, LANES), 0)).astype(jnp.float32)
    for target in (send_ref, keep_ref):
        target[RESP:, :] = jnp.zeros((requests, tp_size * chunk), jnp.float32)
    for digit in range(3):
        value = ((own_targets >> (8 * digit)) & 255).astype(jnp.float32)
        value = jnp.dot(value, spread, preferred_element_type=jnp.float32)
        lanes = slice(2 * chunk + digit * LANES, 2 * chunk + (digit + 1) * LANES)
        for target in (send_ref, keep_ref):
            target[RESP:, lanes] = value
    starts = offsets_of(lengths, requests)
    column = lax.broadcasted_iota(jnp.int32, index_ref.shape, 1)
    source = jnp.zeros(index_ref.shape, jnp.int32)
    for at, k in enumerate(order):
        source = jnp.where(column // RESP == at, req_index ^ k, source)
    base = jnp.zeros(index_ref.shape, jnp.int32)
    count = jnp.zeros(index_ref.shape, jnp.int32)
    per_device = code_ref.shape[0]
    row = tp_index // 2 * per_device + lax.broadcasted_iota(jnp.int32, code_ref.shape, 0)
    code = jnp.zeros(code_ref.shape, jnp.int32)
    own_start, own_count = jnp.int32(0), jnp.int32(1)
    for i in range(requests):
        base = jnp.where(source == i, starts[i], base)
        count = jnp.where(source == i, lengths[i], count)
        code = jnp.where(row >= starts[i], row - starts[i] + i * RESP, code)
        own_start = jnp.where(owners[i] == req_index, starts[i], own_start)
        own_count = jnp.where(owners[i] == req_index, lengths[i], own_count)
    index_ref[...] = jnp.where(column % RESP < count, base + column % RESP, -1)
    code_ref[...] = code
    lane = lax.broadcasted_iota(jnp.int32, span_ref.shape, 1)
    span_ref[...] = jnp.where(lane == 0, own_start, own_count)


def logits_kernel(tp_size, block, index_ref, rows_ref, gain_ref, head_ref, got_ref, sent_ref, keep_ref):
    tp_index = lax.axis_index("tp")
    step = pl.program_id(0)
    wide = index_ref.shape[1]
    total = tp_size * block
    per_block = wide * 5 // 8 // tp_size
    pair = tp_index // 2
    row = lax.broadcasted_iota(jnp.int32, (total, 1), 0)
    wanted = jnp.zeros((total, 1), jnp.int32)
    for place in range(tp_size):
        first = (2 * (pair ^ (1 - place // 2)) + place % 2) * per_block + step * block - place * block
        wanted = jnp.where(row // block == place, row + first, wanted)
    pick = (wanted == index_ref[...]).astype(jnp.float32).astype(jnp.bfloat16)
    vocab, chunk = got_ref.shape
    rows = rows_ref[...].reshape(wide, 2 * chunk)
    live = jnp.dot(pick, rows, preferred_element_type=jnp.float32)
    bare = live * (1.0 / gain_ref[...])
    square = jnp.broadcast_to(jnp.sum(bare * bare, axis=1, keepdims=True), (total, LANES))
    live = live.astype(jnp.bfloat16)
    contract_last = (((1,), (1,)), ((), ()))
    head = jnp.concatenate([head_ref[tp_index % 2], got_ref[...]], axis=1)
    logits = lax.dot_general(live, head, contract_last, preferred_element_type=jnp.float32)
    lane = lax.broadcasted_iota(jnp.int32, (block, LANES), 1)
    for place in range(tp_size):
        span = slice(place * block, (place + 1) * block)
        body, whole = logits[span], square[span]
        if place // 2:
            keep_ref[place % 2, :, 0:vocab] = body
            keep_ref[place % 2, :, vocab : vocab + LANES] = whole
            continue
        coarse = body.astype(jnp.bfloat16).astype(jnp.float32)
        size = jnp.abs(body)
        top = jnp.max(size, axis=1, keepdims=True)
        rest = jnp.max(jnp.where(size == top, body - coarse, -jnp.inf), axis=1, keepdims=True)
        high = whole.astype(jnp.bfloat16).astype(jnp.float32)
        tail = jnp.where(lane == 0, high, whole - high)
        tail = jnp.where(lane == 2, rest, tail)
        tail = jnp.where(lane == 3, top, tail)
        sent_ref[place % 2, :, 0:vocab] = coarse
        sent_ref[place % 2, :, vocab : vocab + LANES] = tail


def lse_kernel(m, width, keep_ref, last_ref, targets_ref, code_ref, *refs):
    stats_ref = refs[-1]
    req_index = lax.axis_index("req")
    block = code_ref.shape[0]
    vocab = keep_ref.shape[2] - LANES
    requests = targets_ref.shape[0]
    code = code_ref[...]
    lane = lax.broadcasted_iota(jnp.int32, (block, LANES), 1)
    digits = jnp.zeros((block, LANES), jnp.float32)
    for i in range(requests):
        here = (
            targets_ref[i : i + 1, 0:LANES]
            + targets_ref[i : i + 1, LANES : 2 * LANES] * 256.0
            + targets_ref[i : i + 1, 2 * LANES : 3 * LANES] * 65536.0
        )
        digits = digits + jnp.where(code == i * RESP + lane, jnp.where(lane < RESP, here, 0.0), 0.0)
    wanted = jnp.sum(digits, axis=1, keepdims=True).astype(jnp.int32) - req_index * vocab
    near = keep_ref[0]
    tail = last_ref[:, vocab : vocab + LANES]
    column = lax.broadcasted_iota(jnp.int32, (block, vocab), 1)
    last = last_ref[:, 0:vocab]
    logits = near[:, 0:vocab] + last + jnp.where(jnp.abs(last) == tail[:, 3:4], tail[:, 2:3], 0.0)
    square = near[:, vocab : vocab + 1] + tail[:, 0:1] + tail[:, 1:2]
    logits = logits * lax.rsqrt(square / width + 1e-06)
    peak = jnp.max(logits, axis=1, keepdims=True)
    lse = peak + jnp.log(jnp.sum(jnp.exp(logits - peak), axis=1, keepdims=True))
    picked = jnp.sum(jnp.where(column == wanted, logits, 0.0), axis=1, keepdims=True)
    stats = jnp.where(lane == 0, lse, jnp.where(lane == 1, picked, 0.0))
    if m:
        space = jnp.zeros((LANES // 2 - block, LANES), jnp.float32)
        stats = jnp.concatenate([refs[0][...], space, stats, space], axis=0)
        stats = jnp.broadcast_to(stats.T[0:2], stats_ref.shape)
    stats_ref[...] = stats


def final_kernel(tp_size, block, per_device, span_ref, stats_ref, policy_ref, scores_ref):
    tp_index = lax.axis_index("tp")
    step = pl.program_id(0)
    quarter = policy_ref.shape[1]
    stats = stats_ref[...].reshape((-1, tp_size) + stats_ref.shape[1:])
    peak = jnp.max(stats[:, :, 0:1], axis=0)
    whole = peak + jnp.log(jnp.sum(jnp.exp(stats[:, :, 0:1] - peak), axis=0))
    logprob = jnp.sum(stats[:, :, 1:2], axis=0) - whole
    start = span_ref[0:1, 0:1]
    count = span_ref[0:1, 1:2]
    lane = lax.broadcasted_iota(jnp.int32, (1, LANES), 1)
    inner = lane % (LANES // 2)
    own = tp_index * quarter + lax.broadcasted_iota(jnp.int32, (quarter, 1), 0)
    policy = jnp.zeros((quarter, 1), jnp.float32)
    total = jnp.zeros((1, 1), jnp.float32)
    ratio = jnp.zeros((1, 1), jnp.float32)
    part = jnp.where(lane < LANES // 2, 0, 1)
    for t in range(tp_size):
        slot = (t // 2 * 2 + part) * per_device + step * block + inner - start
        live = (inner < block) & (slot >= 0) & (slot < count)
        value = jnp.where(live, logprob[t], 0.0)
        if t % 2:
            ratio = ratio - jnp.sum(value, axis=1, keepdims=True)
        else:
            policy = policy + jnp.sum(
                jnp.where(live & (slot == own), value, 0.0), axis=1, keepdims=True
            )
            total = total + jnp.sum(value, axis=1, keepdims=True)
            ratio = ratio + jnp.sum(value, axis=1, keepdims=True)
    eye = lax.broadcasted_iota(jnp.int32, (quarter, quarter), 0) == lax.broadcasted_iota(
        jnp.int32, (quarter, quarter), 1
    )
    policy = jnp.sum(jnp.where(eye, policy, 0.0), axis=0, keepdims=True)
    divisor = count.astype(jnp.float32)
    lane = lax.broadcasted_iota(jnp.int32, (1, 2), 1)
    scores = jnp.where(lane == 0, total / divisor, ratio / divisor)

    @pl.when(step == 0)
    def _():
        policy_ref[...] = policy
        scores_ref[...] = scores

    @pl.when(step > 0)
    def _():
        policy_ref[...] += policy
        scores_ref[...] += scores


def per_device(
    queries,
    response_kv,
    cache_kv,
    residual,
    out_proj,
    norm_gain,
    lm_head,
    targets,
    resp_lengths,
    cache_lengths,
    owner_slot,
    sink_count,
    window_size,
):
    tp_size = lax.axis_size("tp")
    requests = targets.shape[0]
    quarter = RESP // tp_size
    width = residual.shape[3]
    chunk = width // tp_size
    per_block = requests * RESP * 5 // 8 // tp_size
    f32, bf16, i32 = jnp.float32, jnp.bfloat16, jnp.int32
    order = gather_order(lax.axis_size("req"))
    packed = jax.ShapeDtypeStruct((RESP + requests, width), f32)
    send, keep, own_gain, index, code, span = pl.pallas_call(
        functools.partial(attend_kernel, tp_size, order),
        out_shape=(
            packed,
            packed,
            jax.ShapeDtypeStruct((1, 2 * chunk), f32),
            jax.ShapeDtypeStruct((1, requests * RESP), i32),
            jax.ShapeDtypeStruct((2 * per_block, LANES), i32),
            jax.ShapeDtypeStruct((1, LANES), i32),
        ),
        in_specs=[SMEM] * 3 + [HBM] * 9,
        out_specs=(VMEM,) * 6,
        scratch_shapes=[
            pltpu.SMEM((requests,), i32),
            pltpu.SMEM((requests,), i32),
            pltpu.VMEM((2, RESP, queries.shape[3]), bf16),
            pltpu.VMEM(targets.shape, i32),
            pltpu.VMEM((RESP, 2 * chunk), bf16),
            pltpu.VMEM((1, 2 * chunk), f32),
            pltpu.VMEM((2, 2, RESP, HEAD), bf16),
            pltpu.VMEM((2, 2, CACHE, HEAD), bf16),
            pltpu.VMEM(out_proj.shape, bf16),
            pltpu.SemaphoreType.DMA((8 + 2,)),
        ],
        compiler_params=pltpu.CompilerParams(vmem_limit_bytes=16 * MIB),
        name="attend",
    )(
        cache_lengths,
        sink_count,
        window_size,
        *[
            pltpu.with_memory_space_constraint(operand, pltpu.HBM)
            for operand in (
                resp_lengths,
                owner_slot,
                queries,
                targets,
                residual,
                norm_gain,
                response_kv,
                cache_kv,
                out_proj,
            )
        ]
    )
    head, send = lax.optimization_barrier((lm_head, send))
    head = lax.dynamic_index_in_dim(head, 1 - lax.axis_index("tp") % 2, axis=0, keepdims=False)
    head = swap(head, "tp", 1)
    whole = keep + swap(send.astype(bf16), "tp", 1).astype(f32)
    got = swap(whole[:, 2 * chunk :].astype(bf16), "tp", 2).astype(f32)
    riders = whole[RESP:, 2 * chunk : 2 * chunk + 3 * LANES] + got[RESP:, : 3 * LANES]
    scaled = ((whole[:RESP, : 2 * chunk] + got[:RESP]) * own_gain).astype(bf16)
    steps = max(1, requests // 8)
    block = per_block // steps
    vocab = lm_head.shape[1]
    flat = pl.BlockSpec((block, vocab + LANES), lambda g: (g, 0))
    slab = pl.BlockSpec((block, LANES), lambda g: (g, 0))
    rows = scaled[None]
    *groups, longest, _ = exchange_steps(lax.axis_size("req"))
    for group in groups:
        rows = jnp.concatenate([rows] + [swap(rows, "req", step) for step in group], axis=0)
    got = [swap(rows, "req", step) for step in longest]
    side = swap(rows, "req", 1)
    far = [swap(got[0], "req", 1), swap(jnp.concatenate(got[1:], axis=0), "req", 1)]
    rows = jnp.concatenate([rows] + got + [side] + far, axis=0)
    packed = jax.ShapeDtypeStruct((2, per_block, vocab + LANES), f32)
    spec = pl.BlockSpec((2, block, vocab + LANES), lambda g: (0, g, 0))
    sent, keep = pl.pallas_call(
        functools.partial(logits_kernel, tp_size, block),
        out_shape=(packed, packed),
        grid=(steps,),
        in_specs=[VMEM] * 5,
        out_specs=(spec, spec),
        compiler_params=pltpu.CompilerParams(vmem_limit_bytes=32 * MIB),
        cost_estimate=BRIEF,
        name="logits",
    )(index, rows, own_gain, lm_head, head)
    parts = [swap(sent[i].astype(bf16), "tp", 2).astype(f32) for i in range(2)]
    everyone = lax.axis_size("req") * tp_size
    wide = pl.BlockSpec((everyone, 2, LANES), lambda g: (0, 0, g))
    stats = []
    for m, last in enumerate(parts):
        shape = (everyone, 2, steps * LANES) if m else (per_block, LANES)
        stats = [
            pl.pallas_call(
                functools.partial(lse_kernel, m, width),
                out_shape=jax.ShapeDtypeStruct(shape, f32),
                grid=(steps,),
                in_specs=[
                    pl.BlockSpec((1, block, vocab + LANES), lambda g, m=m: (m, g, 0)),
                    flat,
                    VMEM,
                    pl.BlockSpec((block, LANES), lambda g, m=m: (m * steps + g, 0)),
                ]
                + [slab] * m,
                out_specs=wide if m else slab,
                compiler_params=pltpu.CompilerParams(vmem_limit_bytes=16 * MIB),
                cost_estimate=BRIEF,
                name="lse",
            )(keep, last, riders, code, *stats)
        ]
    stats = lax.all_to_all(stats[0], ("req", "tp"), 0, 0, tiled=True)
    return pl.pallas_call(
        functools.partial(final_kernel, tp_size, block, per_block),
        out_shape=(
            jax.ShapeDtypeStruct((1, quarter), f32),
            jax.ShapeDtypeStruct((1, 2), f32),
        ),
        grid=(steps,),
        in_specs=[VMEM, wide],
        out_specs=(VMEM, VMEM),
        compiler_params=pltpu.CompilerParams(vmem_limit_bytes=8 * MIB),
        name="final",
    )(span, stats)


def solution(mesh):
    in_specs = (
        P(None, "req", None, "tp"),
        P(None, "req", None, None, None),
        P(None, "req", None, None, None),
        P(None, "req", None, None),
        P(None, "tp", None),
        P(),
        P(None, "req", "tp"),
        P(None, "tp"),
        P(),
        P("req"),
        P(),
        P(),
        P(),
    )
    out_specs = (P("req", "tp"), P("req", None))
    return jax.shard_map(
        per_device, mesh=mesh, in_specs=in_specs, out_specs=out_specs, check_vma=False
    )
```
